32 devices in a mesh: groups: 2 (over x), heads: 16 (over z, y, core).
Axes of the slice: x: 2, y: 2, z: 4, core: 2. Of those that a mesh axis runs over, the one named last changes fastest.
Arguments:
- q_codes: bfloat16 [1536, 6, 2048], P('heads', 'groups'), parts along dimension 1, may hold values from -6 to 6
- k_codes: bfloat16 [512, 6, 2048], P('heads', 'groups'), parts along dimension 1, may hold values from -6 to 6
- q_exps: int32 [6, 12, 16], P('groups'), parts along dimension 0, may hold values from -4 to -1
- k_exps: int32 [6, 4, 16], P('groups'), parts along dimension 0, may hold values from -4 to -1
- shard_of_host: int32 [16], replicated, may hold values from 0 to 15, each once
- head_owner: int32 [16], replicated, may hold values from 0 to 15, each once
Outputs:
- absorbed: bfloat16 [32, 6, 1536, 512], P('heads', 'groups'), parts along dimension 1
The draws below stay inside these ranges and needn't reach their ends.
There are 2 independent parts, one for each index of `groups`. The reference program is written for one: setup_inputs(seed, part) draws one part's arguments, and reference() takes and returns one part's arrays. A program takes and returns all parts, laid end to end along the dimension named above; an argument that names none is the same for every part. Nothing has to cross between parts.
Inputs may be any that keep to these rules, and one draw needn't show every extreme that they name: `shard_of_host`: each shard is held by exactly one host. `head_owner`: each device owns exactly one head.
All inputs are finite; a program needn't handle non-finite values.
Results may differ from the reference program's by a relative error of at most 0.001.
Values may be sent and summed in bfloat16 or wider, within the bound.
A program may use at most 64 MiB of HBM per device.

```python
import jax
import jax.numpy as jnp
from jax import lax

QR = 1536
KVR = 512
HD = 128
BLK = 128
LAYERS = 3
HEADS = 16


def plant(drawn, rng, low, high):
    place = [jax.random.randint(jax.random.fold_in(rng, axis), (), 0, length) for axis, length in enumerate(drawn.shape)]
    longest = drawn.shape.index(max(drawn.shape))
    next_to = place[:longest] + [(place[longest] + 1) % drawn.shape[longest]] + place[longest + 1:]
    return drawn.at[tuple(place)].set(low).at[tuple(next_to)].set(high)


def block_levels(rng, dims, split, least, largest):
    gain = 1.0
    for axis_at, parts in split:
        heights = jax.random.uniform(jax.random.fold_in(jax.random.fold_in(rng, 6), axis_at), (parts,), jnp.float32, least / len(split), largest / len(split))
        gain = gain * jnp.repeat(jnp.exp(heights), dims[axis_at] // parts).reshape((-1,) + (1,) * (len(dims) - 1 - axis_at))
    return gain


def noise(rng, dims, scale, limit, shards=(), held_as=jnp.bfloat16):
    result = scale * jax.random.normal(rng, dims, jnp.float32)
    if shards:
        result = result * block_levels(rng, dims, shards, -0.22, 0.18)
    return jnp.clip(result, -limit, limit).astype(held_as)


def setup_inputs(seed: int = 0, part: int = 0) -> dict:
    arg_keys = jax.random.split(jax.random.key(seed), 7)
    own_keys = jax.random.split(jax.random.fold_in(arg_keys[6], part), 7)
    return {
        "q_codes": noise(own_keys[0], (QR, LAYERS, HEADS * HD), 1.0, 6.0, ((0, 16),)),
        "k_codes": noise(own_keys[1], (KVR, LAYERS, HEADS * HD), 1.0, 6.0, ((0, 16),)),
        "q_exps": plant(jax.random.randint(own_keys[2], (LAYERS, QR // BLK, HEADS), -4, 0), jax.random.fold_in(own_keys[2], 1), -4, -1).astype(jnp.int32),
        "k_exps": plant(jax.random.randint(own_keys[3], (LAYERS, KVR // BLK, HEADS), -4, 0), jax.random.fold_in(own_keys[3], 1), -4, -1).astype(jnp.int32),
        "shard_of_host": jax.random.permutation(arg_keys[4], HEADS).astype(jnp.int32),
        "head_owner": jax.random.permutation(arg_keys[5], HEADS).astype(jnp.int32),
    }


def to_file(codes, shard_of_host):
    hosts = shard_of_host.shape[0]
    rows, layers, width = codes.shape
    holder = jnp.zeros((hosts,), jnp.int32).at[shard_of_host].set(jnp.arange(hosts, dtype=jnp.int32))
    blocks = codes.reshape(hosts, rows // hosts, layers, width)
    return jnp.take(blocks, holder, axis=0).reshape(rows, layers, width)


def dequant(codes, exps):
    rows, layers, width = codes.shape
    heads = exps.shape[2]
    scale = jnp.exp2(exps.astype(jnp.float32))
    scale = jnp.repeat(scale, rows // exps.shape[1], axis=1).transpose(1, 0, 2)
    values = codes.astype(jnp.float32).reshape(rows, layers, heads, width // heads)
    return (values * scale[..., None]).astype(jnp.bfloat16)


def reference(q_codes, k_codes, q_exps, k_exps, shard_of_host, head_owner):
    q_weight = dequant(to_file(q_codes, shard_of_host), q_exps)
    k_weight = dequant(to_file(k_codes, shard_of_host), k_exps)
    count = head_owner.shape[0]
    half = count // 2

    def one_head(head):
        q_part = jnp.take(q_weight, head, axis=2).astype(jnp.float32)
        k_part = jnp.take(k_weight, head, axis=2).astype(jnp.float32)
        return jnp.einsum("qld,kld->lqk", q_part, k_part).astype(jnp.bfloat16)

    head_mat = lax.map(one_head, jnp.arange(count, dtype=jnp.int32))
    owned = jnp.zeros((count,), jnp.int32).at[head_owner].set(jnp.arange(count, dtype=jnp.int32))
    lower = jnp.arange(count, dtype=jnp.int32) % half
    slot_heads = jnp.stack([owned[lower], owned[lower + half]], axis=1).reshape(2 * count)
    return jnp.take(head_mat, slot_heads, axis=0)
```

```python
import functools
import math

import jax
import jax.numpy as jnp
from jax import lax
from jax.experimental import pallas as pl
from jax.experimental.pallas import tpu as pltpu
from jax.sharding import PartitionSpec as P

BLK = 128
MESH = pl.DeviceIdType.MESH


def exchange(n, q_ref, k_ref, table_ref, owned_ref, out_ref, scaled, send_buf, send_sem, recv_sem, own_sem):
    half = n // 2
    me = lax.axis_index("heads")
    layers, q_rows, _ = q_ref.shape
    k_rows = k_ref.shape[1]
    lower = lax.rem(me, half)
    mine = me - lower
    other = half - mine

    barrier = pltpu.get_barrier_semaphore()

    def greet(i, carry):
        pl.semaphore_signal(barrier, inc=1, device_id={"heads": lax.rem(me + i, n)}, device_id_type=MESH)
        return carry

    lax.fori_loop(1, n, greet, 0)
    q_chunks = q_rows // math.gcd(q_rows, BLK)

    def part(ref, layer, head, rows, first):
        unit = math.gcd(rows, BLK)
        values = ref[layer, :, pl.ds(pl.multiple_of(head * 128, 128), 128)].astype(jnp.float32)
        pieces = []
        for c in range(rows // unit):
            expo = table_ref[layer, first + c, head]
            scale = jnp.exp2(jnp.full((8, 128), expo, jnp.int32).astype(jnp.float32))
            piece = values[c * unit : (c + 1) * unit].reshape(unit // 8, 8, 128) * scale[None]
            pieces.append(piece.reshape(unit, 128))
        return pieces

    def weigh(head, carry):
        for layer in range(layers):
            pieces = part(q_ref, layer, head, q_rows, 0) + part(k_ref, layer, head, k_rows, q_chunks)
            scaled[head, layer] = jnp.concatenate(pieces, axis=0).astype(jnp.bfloat16)
        return carry

    lax.fori_loop(0, n, weigh, 0)

    def prepare(t):
        for slot in range(2):
            send_buf[t, slot] = scaled[owned_ref[t + slot * half]]

    def remote(t, to):
        return pltpu.make_async_remote_copy(
            src_ref=send_buf.at[t],
            dst_ref=out_ref.at[me],
            send_sem=send_sem.at[to],
            recv_sem=recv_sem.at[me],
            device_id={"heads": to},
            device_id_type=MESH,
        )

    prepare(lower)
    pl.semaphore_wait(barrier, n - 1)
    remote(lower, lower + other).start()
    own = pltpu.make_async_copy(send_buf.at[lower], out_ref.at[me], own_sem)
    own.start()

    def far(i, carry):
        t = lax.rem(lower + i, half)
        prepare(t)
        remote(t, t + other).start()
        return carry

    lax.fori_loop(1, half, far, 0)

    def near(i, carry):
        t = lax.rem(lower + i, half)
        remote(t, t + mine).start()
        return carry

    lax.fori_loop(1, half, near, 0)

    def finish(i, carry):
        peer = lax.rem(me + i, n)
        copy = pltpu.make_async_remote_copy(
            src_ref=send_buf.at[lax.rem(peer, half)],
            dst_ref=out_ref.at[peer],
            send_sem=send_sem.at[peer],
            recv_sem=recv_sem.at[peer],
            device_id={"heads": peer},
            device_id_type=MESH,
        )
        copy.wait_send()
        copy.wait_recv()
        return carry

    lax.fori_loop(1, n, finish, 0)
    own.wait()


def absorb(n, q_rows, k_rows, splits, shard_ref, recv_ref, out_ref, q_file, k_file):
    @pl.when(pl.program_id(2) == 0)
    def _():
        for host in range(n):
            shard = shard_ref[host]
            block = recv_ref[host, 0, 0].astype(q_file.dtype)
            q_file[pl.ds(pl.multiple_of(shard * q_rows, q_rows), q_rows)] = block[:q_rows]
            k_file[pl.ds(pl.multiple_of(shard * k_rows, k_rows), k_rows)] = block[q_rows:]

    rows = n * q_rows // splits
    at = pl.multiple_of(pl.program_id(2) * rows, rows)
    out_ref[0, 0] = lax.dot_general(
        q_file[pl.ds(at, rows)].astype(jnp.bfloat16),
        k_file[...].astype(jnp.bfloat16),
        (((1,), (1,)), ((), ())),
        preferred_element_type=jnp.float32,
    ).astype(jnp.bfloat16)


def tables(q_rows, k_rows, q_exps, k_exps, shard, head_owner):
    heads = head_owner.shape[0]
    order = jnp.arange(heads, dtype=jnp.int32)
    q_unit, k_unit = math.gcd(q_rows, BLK), math.gcd(k_rows, BLK)
    q_blocks = q_exps.shape[1]
    every = jnp.concatenate([q_exps, k_exps], axis=1)
    blocks = [(shard * q_rows + at) // BLK for at in range(0, q_rows, q_unit)]
    blocks += [q_blocks + (shard * k_rows + at) // BLK for at in range(0, k_rows, k_unit)]
    at_block = jnp.stack(blocks)[:, None] == jnp.arange(every.shape[1], dtype=jnp.int32)[None]
    table = jnp.sum(jnp.where(at_block[None, :, :, None], every[:, None], 0), axis=2, dtype=jnp.int32)
    owned = jnp.sum(jnp.where(order[:, None] == head_owner[None], order[None], 0), axis=1, dtype=jnp.int32)
    return table, owned


def per_device(n, q_codes, k_codes, q_exps, k_exps, shard_of_host, head_owner):
    q_rows, layers, width = q_codes.shape
    k_rows = k_codes.shape[0]
    rows = q_rows + k_rows
    half = n // 2
    shard = shard_of_host[lax.axis_index("heads")]
    table, owned = tables(q_rows, k_rows, q_exps, k_exps, shard, head_owner)
    smem = pl.BlockSpec(memory_space=pltpu.SMEM)
    vmem = pl.BlockSpec(memory_space=pltpu.VMEM)
    received = pl.pallas_call(
        functools.partial(exchange, n),
        out_shape=jax.ShapeDtypeStruct((n, 2, layers, rows, 128), jnp.bfloat16),
        in_specs=[vmem, vmem, smem, smem],
        out_specs=pl.BlockSpec(memory_space=pl.ANY),
        scratch_shapes=[
            pltpu.VMEM((n, layers, rows, 128), jnp.bfloat16),
            pltpu.VMEM((half, 2, layers, rows, 128), jnp.bfloat16),
            pltpu.SemaphoreType.DMA((n,)),
            pltpu.SemaphoreType.DMA((n,)),
            pltpu.SemaphoreType.DMA,
        ],
        compiler_params=pltpu.CompilerParams(
            collective_id=0, has_side_effects=True, vmem_limit_bytes=24 * 2**20
        ),
    )(q_codes.transpose(1, 0, 2), k_codes.transpose(1, 0, 2), table, owned)

    splits = 2
    q_all, k_all = n * q_rows, n * k_rows
    held = jnp.bfloat16 if q_rows % 16 == 0 and k_rows % 16 == 0 else jnp.float32
    return pl.pallas_call(
        functools.partial(absorb, n, q_rows, k_rows, splits),
        out_shape=jax.ShapeDtypeStruct((2, layers, q_all, k_all), jnp.bfloat16),
        grid_spec=pltpu.PrefetchScalarGridSpec(
            num_scalar_prefetch=1,
            grid=(2, layers, splits),
            in_specs=[pl.BlockSpec((n, 1, 1, rows, 128), lambda a, b, c, shard: (0, a, b, 0, 0))],
            out_specs=pl.BlockSpec((1, 1, q_all // splits, k_all), lambda a, b, c, shard: (a, b, c, 0)),
            scratch_shapes=[pltpu.VMEM((q_all, 128), held), pltpu.VMEM((k_all, 128), held)],
        ),
        compiler_params=pltpu.CompilerParams(vmem_limit_bytes=24 * 2**20),
        cost_estimate=pl.CostEstimate(
            flops=2 * 2 * layers * q_all * k_all * 128,
            bytes_accessed=2 * layers * (q_all * k_all + n * rows * 128) * 2,
            transcendentals=0,
        ),
    )(shard_of_host, received)


def solution(mesh):
    placed = (
        P("heads", "groups", None),
        P("heads", "groups", None),
        P("groups", None, None),
        P("groups", None, None),
        P(),
        P(),
    )
    return jax.shard_map(
        functools.partial(per_device, mesh.shape["heads"]),
        mesh=mesh,
        in_specs=placed,
        out_specs=P("heads", "groups", None, None),
        check_vma=False,
    )
```

```python
import functools
import math

import jax
import jax.numpy as jnp
from jax import lax
from jax.experimental import pallas as pl
from jax.experimental.pallas import tpu as pltpu
from jax.sharding import PartitionSpec as P

BLK = 128
LANES = 128
ORDER = 1
MESH = pl.DeviceIdType.MESH
VMEM = pl.BlockSpec(memory_space=pltpu.VMEM)
SMEM = pl.BlockSpec(memory_space=pltpu.SMEM)
HBM = pl.BlockSpec(memory_space=pltpu.HBM)


def position(table_ref, n, value):
    found = jnp.int32(0)
    for at in range(n):
        found = jnp.where(table_ref[at] == value, jnp.int32(at), found)
    return found


def exchange(
    n, q_hbm, k_hbm, qe_ref, ke_ref, shard_ref, owner_ref, out_ref,
    q_in, k_in, q_scaled, k_scaled, q_send, k_send, q_recv, k_recv, k_file,
    in_sem, q_send_sem, k_send_sem, q_recv_sem, k_recv_sem,
):
    half = n // 2
    me = lax.axis_index("heads")
    layers, q_rows, _ = q_in.shape
    k_rows = k_in.shape[1]
    lower = lax.rem(me, half)
    mine = me - lower
    other = half - mine

    loads = [pltpu.make_async_copy(k_hbm, k_in, in_sem.at[0]), pltpu.make_async_copy(q_hbm, q_in, in_sem.at[1])]
    for load in loads:
        load.start()

    barrier = pltpu.get_barrier_semaphore()

    def greet(i, carry):
        pl.semaphore_signal(barrier, inc=1, device_id={"heads": lax.rem(me + i, n)}, device_id_type=MESH)
        return carry

    lax.fori_loop(1, n, greet, 0)

    shard = shard_ref[me]

    def weigh(source, exps_ref, target, rows, head):
        unit = math.gcd(rows, BLK)
        for layer in range(layers):
            values = source[layer, :, pl.ds(pl.multiple_of(head * LANES, LANES), LANES)].astype(jnp.float32)
            pieces = []
            for at in range(0, rows, unit):
                expo = exps_ref[layer, lax.div(shard * rows + at, BLK), head]
                scale = jnp.exp2(jnp.full((8, LANES), expo, jnp.int32).astype(jnp.float32))
                piece = values[at : at + unit].reshape(unit // 8, 8, LANES) * scale[None]
                pieces.append(piece.reshape(unit, LANES))
            target[head, layer] = jnp.concatenate(pieces, axis=0).astype(jnp.bfloat16)

    def weigh_k(head, carry):
        weigh(k_in, ke_ref, k_scaled, k_rows, head)
        return carry

    def weigh_q(head, carry):
        weigh(q_in, qe_ref, q_scaled, q_rows, head)
        return carry

    loads[0].wait()
    lax.fori_loop(0, n, weigh_k, 0)
    loads[1].wait()
    lax.fori_loop(0, n, weigh_q, 0)

    def prepare(t):
        for slot in range(2):
            head = position(owner_ref, n, t + slot * half)
            k_send[t, slot] = k_scaled[head]
            q_send[t, slot] = q_scaled[head]

    def copy(send, recv, send_sem, recv_sem, to, slot):
        return pltpu.make_async_remote_copy(
            src_ref=send.at[lax.rem(to, half)],
            dst_ref=recv.at[slot],
            send_sem=send_sem.at[to],
            recv_sem=recv_sem.at[slot],
            device_id={"heads": to},
            device_id_type=MESH,
        )

    q_copy = functools.partial(copy, q_send, q_recv, q_send_sem, q_recv_sem)
    k_copy = functools.partial(copy, k_send, k_recv, k_send_sem, k_recv_sem)

    prepare(lower)
    pl.semaphore_wait(barrier, n - 1)
    k_copy(lower + other, me).start()
    q_copy(lower + other, me).start()
    k_recv[me] = k_send[lower]
    q_recv[me] = q_send[lower]

    def far(i, carry):
        t = lax.rem(lower + i, half)
        prepare(t)
        k_copy(t + other, me).start()
        if ORDER == 0:
            q_copy(t + other, me).start()
        if ORDER == 1:
            k_copy(t + mine, me).start()
            q_copy(t + other, me).start()
            q_copy(t + mine, me).start()
        if ORDER == 2:
            k_copy(t + mine, me).start()
        return carry

    lax.fori_loop(1, half, far, 0)

    def near(i, carry):
        t = lax.rem(lower + i, half)
        if ORDER == 2:
            q_copy(t + other, me).start()
        if ORDER == 0:
            k_copy(t + mine, me).start()
        q_copy(t + mine, me).start()
        return carry

    if ORDER != 1:
        lax.fori_loop(1, half, near, 0)

    def k_arrival(i, carry):
        k_copy(0, lax.rem(me + i, n)).wait_recv()
        return carry

    lax.fori_loop(1, n, k_arrival, 0)
    holders = [position(shard_ref, n, s) for s in range(n)]
    for slot in range(2):
        for layer in range(layers):
            rows = [k_recv[holder, slot, layer].astype(jnp.float32) for holder in holders]
            k_file[slot, layer] = jnp.concatenate(rows, axis=0).astype(jnp.bfloat16)

    def multiply(host):
        for slot in range(2):
            for layer in range(layers):
                out_ref[host, slot, layer] = lax.dot_general(
                    q_recv[host, slot, layer],
                    k_file[slot, layer],
                    (((1,), (1,)), ((), ())),
                    preferred_element_type=jnp.float32,
                ).astype(jnp.bfloat16)

    def arrival(i, carry):
        here = mine + lax.rem(lower + half - i, half)
        there = other + lax.rem(lower + half - i, half)

        @pl.when(i > 0)
        def _():
            q_copy(0, here).wait_recv()

        multiply(here)
        q_copy(0, there).wait_recv()
        multiply(there)
        return carry

    lax.fori_loop(0, half, arrival, 0)

    def finish(i, carry):
        peer = lax.rem(me + i, n)
        k_copy(peer, 0).wait_send()
        q_copy(peer, 0).wait_send()
        return carry

    lax.fori_loop(1, n, finish, 0)


def place(n, shard_ref, products, out_ref, sem):
    rows = products.shape[3]

    def row_copy(host):
        at = pl.ds(pl.multiple_of(shard_ref[host] * rows, rows), rows)
        return pltpu.make_async_copy(products.at[host], out_ref.at[:, :, at, :], sem.at[host])

    for host in range(n):
        row_copy(host).start()
    for host in range(n):
        row_copy(host).wait()


def per_device(n, q_codes, k_codes, q_exps, k_exps, shard_of_host, head_owner):
    q_rows, layers, width = q_codes.shape
    k_rows = k_codes.shape[0]
    half = n // 2
    q_all, k_all = n * q_rows, n * k_rows
    sent = jnp.bfloat16
    products = pl.pallas_call(
        functools.partial(exchange, n),
        out_shape=pltpu.VMEM((n, 2, layers, q_rows, k_all), jnp.bfloat16),
        in_specs=[HBM, HBM, SMEM, SMEM, SMEM, SMEM],
        out_specs=VMEM,
        scratch_shapes=[
            pltpu.VMEM((layers, q_rows, width), sent),
            pltpu.VMEM((layers, k_rows, width), sent),
            pltpu.VMEM((n, layers, q_rows, LANES), sent),
            pltpu.VMEM((n, layers, k_rows, LANES), sent),
            pltpu.VMEM((half, 2, layers, q_rows, LANES), sent),
            pltpu.VMEM((half, 2, layers, k_rows, LANES), sent),
            pltpu.VMEM((n, 2, layers, q_rows, LANES), sent),
            pltpu.VMEM((n, 2, layers, k_rows, LANES), sent),
            pltpu.VMEM((2, layers, k_all, LANES), sent),
            pltpu.SemaphoreType.DMA((2,)),
            pltpu.SemaphoreType.DMA((n,)),
            pltpu.SemaphoreType.DMA((n,)),
            pltpu.SemaphoreType.DMA((n,)),
            pltpu.SemaphoreType.DMA((n,)),
        ],
        compiler_params=pltpu.CompilerParams(
            collective_id=0, has_side_effects=True, vmem_limit_bytes=40 * 2**20
        ),
    )(q_codes.transpose(1, 0, 2), k_codes.transpose(1, 0, 2), q_exps, k_exps, shard_of_host, head_owner)

    if q_rows % 16:
        order = jnp.arange(n, dtype=jnp.int32)
        holder = jnp.zeros((n,), jnp.int32).at[shard_of_host].set(order)
        filed = jnp.take(products, holder, axis=0)
        return filed.transpose(1, 2, 0, 3, 4).reshape(2, layers, q_all, k_all)
    return pl.pallas_call(
        functools.partial(place, n),
        out_shape=jax.ShapeDtypeStruct((2, layers, q_all, k_all), jnp.bfloat16),
        in_specs=[SMEM, VMEM],
        out_specs=HBM,
        scratch_shapes=[pltpu.SemaphoreType.DMA((n,))],
        compiler_params=pltpu.CompilerParams(vmem_limit_bytes=40 * 2**20),
    )(shard_of_host, products)


def solution(mesh):
    placed = (
        P("heads", "groups", None),
        P("heads", "groups", None),
        P("groups", None, None),
        P("groups", None, None),
        P(),
        P(),
    )
    return jax.shard_map(
        functools.partial(per_device, mesh.shape["heads"]),
        mesh=mesh,
        in_specs=placed,
        out_specs=P("heads", "groups", None, None),
        check_vma=False,
    )
```

```python
import functools
import math

import jax
import jax.numpy as jnp
from jax import lax
from jax.experimental import pallas as pl
from jax.experimental.pallas import tpu as pltpu
from jax.sharding import PartitionSpec as P

BLK = 128
LANES = 128
STRIDE = 2
SPARE = 2**19
MESH = pl.DeviceIdType.MESH
VMEM = pl.BlockSpec(memory_space=pltpu.VMEM)
SMEM = pl.BlockSpec(memory_space=pltpu.SMEM)
HBM = pl.BlockSpec(memory_space=pltpu.HBM)


def position(table_ref, n, value):
    found = jnp.int32(0)
    for at in range(n):
        found = jnp.where(table_ref[at] == value, jnp.int32(at), found)
    return found


def exchange(
    n, q_hbm, k_hbm, qe_hbm, ke_hbm, shard_hbm, owner_hbm, out_ref,
    qe_ref, ke_ref, shard_ref, owner_ref, q_in, k_in, q_scaled, k_scaled, q_send, k_send, q_recv, k_recv, k_file,
    in_sem, q_send_sem, k_send_sem, q_recv_sem, k_recv_sem,
):
    half = n // 2
    me = lax.axis_index("heads")
    layers, q_rows, _ = q_in.shape
    k_rows = k_in.shape[1]
    lower = lax.rem(me, half)
    mine = me - lower
    other = half - mine

    barrier = pltpu.get_barrier_semaphore()

    def greet(i, carry):
        pl.semaphore_signal(barrier, inc=1, device_id={"heads": lax.rem(me + i, n)}, device_id_type=MESH)
        return carry

    lax.fori_loop(1, n, greet, 0)

    def load(at, source, target):
        copy = pltpu.make_async_copy(source, target, in_sem.at[at])
        copy.start()
        return copy

    k_load = load(0, k_hbm, k_in)
    shard_load = load(1, shard_hbm, shard_ref)
    ke_load = load(2, ke_hbm, ke_ref)
    owner_load = load(3, owner_hbm, owner_ref)
    qe_load = load(4, qe_hbm, qe_ref)
    q_load = load(5, q_hbm, q_in)
    shard_load.wait()
    shard = shard_ref[me]

    def weigh(source, exps_ref, target, rows, head):
        unit = math.gcd(rows, BLK)
        for layer in range(layers):
            values = source[layer, :, pl.ds(pl.multiple_of(head * LANES, LANES), LANES)].astype(jnp.float32)
            pieces = []
            for at in range(0, rows, unit):
                expo = exps_ref[layer, lax.div(shard * rows + at, BLK), head]
                scale = jnp.exp2(jnp.full((8, LANES), expo, jnp.int32).astype(jnp.float32))
                piece = values[at : at + unit].reshape(unit // 8, 8, LANES) * scale[None]
                pieces.append(piece.reshape(unit, LANES))
            target[head, layer] = jnp.concatenate(pieces, axis=0).astype(jnp.bfloat16)

    def weigh_k(head, carry):
        weigh(k_in, ke_ref, k_scaled, k_rows, head)
        return carry

    def weigh_q(head, carry):
        weigh(q_in, qe_ref, q_scaled, q_rows, head)
        return carry

    def prepare(scaled, send, t):
        for slot in range(2):
            send[t, slot] = scaled[position(owner_ref, n, t + slot * half)]

    def copy(send, recv, send_sem, recv_sem, to, slot):
        return pltpu.make_async_remote_copy(
            src_ref=send.at[lax.rem(to, half)],
            dst_ref=recv.at[slot],
            send_sem=send_sem.at[to],
            recv_sem=recv_sem.at[slot],
            device_id={"heads": to},
            device_id_type=MESH,
        )

    q_copy = functools.partial(copy, q_send, q_recv, q_send_sem, q_recv_sem)
    k_copy = functools.partial(copy, k_send, k_recv, k_send_sem, k_recv_sem)

    ke_load.wait()
    k_load.wait()
    lax.fori_loop(0, n, weigh_k, 0)
    owner_load.wait()
    prepare(k_scaled, k_send, lower)
    pl.semaphore_wait(barrier, n - 1)
    k_copy(lower + other, me).start()
    k_recv[me] = k_send[lower]

    def apart(i):
        return lax.rem(i * STRIDE, half) + i * STRIDE // half

    def k_step(i, carry):
        t = lax.rem(lower + apart(i), half)
        prepare(k_scaled, k_send, t)
        k_copy(t + other, me).start()
        k_copy(t + mine, me).start()
        return carry

    lax.fori_loop(1, half, k_step, 0)

    qe_load.wait()
    q_load.wait()
    lax.fori_loop(0, n, weigh_q, 0)
    prepare(q_scaled, q_send, lower)
    q_copy(lower + other, me).start()
    q_recv[me] = q_send[lower]

    def q_step(i, carry):
        t = lax.rem(lower + apart(i), half)
        prepare(q_scaled, q_send, t)
        q_copy(t + other, me).start()
        q_copy(t + mine, me).start()
        return carry

    lax.fori_loop(1, half, q_step, 0)

    def k_arrival(i, carry):
        k_copy(0, lax.rem(me + i, n)).wait_recv()
        return carry

    lax.fori_loop(1, n, k_arrival, 0)
    holders = [position(shard_ref, n, s) for s in range(n)]
    for slot in range(2):
        for layer in range(layers):
            rows = [k_recv[holder, slot, layer].astype(jnp.float32) for holder in holders]
            k_file[slot, layer] = jnp.concatenate(rows, axis=0).astype(jnp.bfloat16)

    def multiply(host):
        for slot in range(2):
            for layer in range(layers):
                out_ref[host, slot, layer] = lax.dot_general(
                    q_recv[host, slot, layer],
                    k_file[slot, layer],
                    (((1,), (1,)), ((), ())),
                    preferred_element_type=jnp.float32,
                ).astype(jnp.bfloat16)

    def arrival(i, carry):
        here = mine + lax.rem(lower + half - apart(i), half)
        there = other + lax.rem(lower + half - apart(i), half)

        @pl.when(i > 0)
        def _():
            q_copy(0, here).wait_recv()

        multiply(here)
        q_copy(0, there).wait_recv()
        multiply(there)
        return carry

    lax.fori_loop(0, half, arrival, 0)

    def finish(i, carry):
        peer = lax.rem(me + i, n)
        k_copy(peer, 0).wait_send()
        q_copy(peer, 0).wait_send()
        return carry

    lax.fori_loop(1, n, finish, 0)


def place(n, shard_ref, products, out_ref, sem):
    rows = products.shape[3]
    for host in range(n):
        at = pl.ds(pl.multiple_of(shard_ref[host] * rows, rows), rows)
        for slot in range(2):
            for layer in range(products.shape[2]):
                pltpu.make_async_copy(products.at[host, slot, layer], out_ref.at[slot, layer, at], sem).start()
    pltpu.make_async_copy(out_ref, out_ref, sem).wait()


def per_device(n, q_codes, k_codes, q_exps, k_exps, shard_of_host, head_owner):
    q_rows, layers, width = q_codes.shape
    k_rows = k_codes.shape[0]
    half = n // 2
    q_all, k_all = n * q_rows, n * k_rows
    sent = jnp.bfloat16
    held = n * 2 * layers * -(-q_rows // 16) * 16 * k_all * 2
    products = pl.pallas_call(
        functools.partial(exchange, n),
        out_shape=pltpu.VMEM((n, 2, layers, q_rows, k_all), jnp.bfloat16),
        in_specs=[HBM] * 6,
        out_specs=VMEM,
        scratch_shapes=[
            pltpu.SMEM(q_exps.shape, jnp.int32),
            pltpu.SMEM(k_exps.shape, jnp.int32),
            pltpu.SMEM((n,), jnp.int32),
            pltpu.SMEM((n,), jnp.int32),
            pltpu.VMEM((layers, q_rows, width), sent),
            pltpu.VMEM((layers, k_rows, width), sent),
            pltpu.VMEM((n, layers, q_rows, LANES), sent),
            pltpu.VMEM((n, layers, k_rows, LANES), sent),
            pltpu.VMEM((half, 2, layers, q_rows, LANES), sent),
            pltpu.VMEM((half, 2, layers, k_rows, LANES), sent),
            pltpu.VMEM((n, 2, layers, q_rows, LANES), sent),
            pltpu.VMEM((n, 2, layers, k_rows, LANES), sent),
            pltpu.VMEM((2, layers, k_all, LANES), sent),
            pltpu.SemaphoreType.DMA((6,)),
            pltpu.SemaphoreType.DMA((n,)),
            pltpu.SemaphoreType.DMA((n,)),
            pltpu.SemaphoreType.DMA((n,)),
            pltpu.SemaphoreType.DMA((n,)),
        ],
        compiler_params=pltpu.CompilerParams(
            collective_id=0, has_side_effects=True, vmem_limit_bytes=64 * 2**20 - held - SPARE
        ),
    )(q_codes.transpose(1, 0, 2), k_codes.transpose(1, 0, 2), q_exps, k_exps, shard_of_host, head_owner)

    if q_rows % 16:
        order = jnp.arange(n, dtype=jnp.int32)
        holder = jnp.zeros((n,), jnp.int32).at[shard_of_host].set(order)
        filed = jnp.take(products, holder, axis=0)
        return filed.transpose(1, 2, 0, 3, 4).reshape(2, layers, q_all, k_all)
    return pl.pallas_call(
        functools.partial(place, n),
        out_shape=jax.ShapeDtypeStruct((2, layers, q_all, k_all), jnp.bfloat16),
        in_specs=[SMEM, VMEM],
        out_specs=HBM,
        scratch_shapes=[pltpu.SemaphoreType.DMA],
        compiler_params=pltpu.CompilerParams(vmem_limit_bytes=40 * 2**20),
    )(shard_of_host, products)


def solution(mesh):
    placed = (
        P("heads", "groups", None),
        P("heads", "groups", None),
        P("groups", None, None),
        P("groups", None, None),
        P(),
        P(),
    )
    return jax.shard_map(
        functools.partial(per_device, mesh.shape["heads"]),
        mesh=mesh,
        in_specs=placed,
        out_specs=P("heads", "groups", None, None),
        check_vma=False,
    )
```

```python
import functools
import math

import jax
import jax.numpy as jnp
from jax import lax
from jax.experimental import pallas as pl
from jax.experimental.pallas import tpu as pltpu
from jax.sharding import PartitionSpec as P

BLK = 128
LANES = 128
STRIDE = 2
SPARE = 2**19
MESH = pl.DeviceIdType.MESH
VMEM = pl.BlockSpec(memory_space=pltpu.VMEM)
SMEM = pl.BlockSpec(memory_space=pltpu.SMEM)
HBM = pl.BlockSpec(memory_space=pltpu.HBM)


def position(table_ref, n, value):
    found = jnp.int32(0)
    for at in range(n):
        found = jnp.where(table_ref[at] == value, jnp.int32(at), found)
    return found


def exchange(
    n, q_hbm, k_hbm, qe_hbm, ke_hbm, shard_hbm, owner_hbm, out_ref,
    qe_ref, ke_ref, shard_ref, owner_ref, q_in, k_in, q_scaled, k_scaled, q_send, k_send, q_recv, k_recv, k_file,
    in_sem, q_send_sem, k_send_sem, q_recv_sem, k_recv_sem,
):
    half = n // 2
    me = lax.axis_index("heads")
    layers, q_rows, _ = q_in.shape
    k_rows = k_in.shape[1]
    lower = lax.rem(me, half)
    mine = me - lower
    other = half - mine

    barrier = pltpu.get_barrier_semaphore()

    def greet(i, carry):
        pl.semaphore_signal(barrier, inc=1, device_id={"heads": lax.rem(me + i, n)}, device_id_type=MESH)
        return carry

    lax.fori_loop(1, n, greet, 0)

    def load(at, source, target):
        copy = pltpu.make_async_copy(source, target, in_sem.at[at])
        copy.start()
        return copy

    k_load = load(0, k_hbm, k_in)
    shard_load = load(1, shard_hbm, shard_ref)
    ke_load = load(2, ke_hbm, ke_ref)
    owner_load = load(3, owner_hbm, owner_ref)
    qe_load = load(4, qe_hbm, qe_ref)
    q_load = load(5, q_hbm, q_in)
    shard_load.wait()
    shard = shard_ref[me]

    def weigh(source, exps_ref, target, rows, head):
        unit = math.gcd(rows, BLK)
        for layer in range(layers):
            values = source[layer, :, pl.ds(pl.multiple_of(head * LANES, LANES), LANES)].astype(jnp.float32)
            pieces = []
            for at in range(0, rows, unit):
                expo = exps_ref[layer, lax.div(shard * rows + at, BLK), head]
                scale = jnp.exp2(jnp.full((8, LANES), expo, jnp.int32).astype(jnp.float32))
                piece = values[at : at + unit].reshape(unit // 8, 8, LANES) * scale[None]
                pieces.append(piece.reshape(unit, LANES))
            target[head, layer] = jnp.concatenate(pieces, axis=0).astype(jnp.bfloat16)

    def weigh_k(head, carry):
        weigh(k_in, ke_ref, k_scaled, k_rows, head)
        return carry

    def weigh_q(head, carry):
        weigh(q_in, qe_ref, q_scaled, q_rows, head)
        return carry

    def prepare(scaled, send, t):
        for slot in range(2):
            send[t, slot] = scaled[position(owner_ref, n, t + slot * half)]

    def copy(send, recv, send_sem, recv_sem, to, slot):
        return pltpu.make_async_remote_copy(
            src_ref=send.at[lax.rem(to, half)],
            dst_ref=recv.at[slot],
            send_sem=send_sem.at[to],
            recv_sem=recv_sem.at[slot],
            device_id={"heads": to},
            device_id_type=MESH,
        )

    q_copy = functools.partial(copy, q_send, q_recv, q_send_sem, q_recv_sem)
    k_copy = functools.partial(copy, k_send, k_recv, k_send_sem, k_recv_sem)

    ke_load.wait()
    k_load.wait()
    lax.fori_loop(0, n, weigh_k, 0)
    owner_load.wait()
    prepare(k_scaled, k_send, lower)
    pl.semaphore_wait(barrier, n - 1)
    k_copy(lower + other, me).start()
    k_recv[me] = k_send[lower]

    def apart(i):
        return lax.rem(i * STRIDE, half) + i * STRIDE // half

    def k_step(i, carry):
        t = lax.rem(lower + apart(i), half)
        prepare(k_scaled, k_send, t)
        k_copy(t + other, me).start()
        k_copy(t + mine, me).start()
        return carry

    lax.fori_loop(1, half, k_step, 0)

    qe_load.wait()
    q_load.wait()
    lax.fori_loop(0, n, weigh_q, 0)
    prepare(q_scaled, q_send, lower)
    q_copy(lower + other, me).start()
    q_recv[me] = q_send[lower]

    def q_step(i, carry):
        t = lax.rem(lower + apart(i), half)
        prepare(q_scaled, q_send, t)
        q_copy(t + other, me).start()
        q_copy(t + mine, me).start()
        return carry

    lax.fori_loop(1, half, q_step, 0)

    def k_arrival(i, carry):
        k_copy(0, lax.rem(me + i, n)).wait_recv()
        k_copy(lax.rem(me + i, n), 0).wait_send()
        return carry

    lax.fori_loop(1, n, k_arrival, 0)
    holders = [position(shard_ref, n, s) for s in range(n)]
    for slot in range(2):
        for layer in range(layers):
            rows = [k_recv[holder, slot, layer].astype(jnp.float32) for holder in holders]
            k_file[slot, layer] = jnp.concatenate(rows, axis=0).astype(jnp.bfloat16)

    def multiply(host):
        for slot in range(2):
            for layer in range(layers):
                out_ref[host, slot, layer] = lax.dot_general(
                    q_recv[host, slot, layer],
                    k_file[slot, layer],
                    (((1,), (1,)), ((), ())),
                    preferred_element_type=jnp.float32,
                ).astype(jnp.bfloat16)

    def arrival(i, carry):
        here = mine + lax.rem(lower + half - apart(i), half)
        there = other + lax.rem(lower + half - apart(i), half)

        @pl.when(i > 0)
        def _():
            q_copy(0, here).wait_recv()

        multiply(here)
        q_copy(0, there).wait_recv()
        multiply(there)
        return carry

    lax.fori_loop(0, half, arrival, 0)

    def finish(i, carry):
        peer = lax.rem(me + i, n)
        q_copy(peer, 0).wait_send()
        return carry

    lax.fori_loop(1, n, finish, 0)


def place(n, shard_ref, products, out_ref, sem):
    rows = products.shape[3]
    for host in range(n):
        at = pl.ds(pl.multiple_of(shard_ref[host] * rows, rows), rows)
        for slot in range(2):
            for layer in range(products.shape[2]):
                pltpu.make_async_copy(products.at[host, slot, layer], out_ref.at[slot, layer, at], sem).start()
    pltpu.make_async_copy(out_ref, out_ref, sem).wait()


def per_device(n, q_codes, k_codes, q_exps, k_exps, shard_of_host, head_owner):
    q_rows, layers, width = q_codes.shape
    k_rows = k_codes.shape[0]
    half = n // 2
    q_all, k_all = n * q_rows, n * k_rows
    sent = jnp.bfloat16
    held = n * 2 * layers * -(-q_rows // 16) * 16 * k_all * 2
    products = pl.pallas_call(
        functools.partial(exchange, n),
        out_shape=pltpu.VMEM((n, 2, layers, q_rows, k_all), jnp.bfloat16),
        in_specs=[HBM] * 6,
        out_specs=VMEM,
        scratch_shapes=[
            pltpu.SMEM(q_exps.shape, jnp.int32),
            pltpu.SMEM(k_exps.shape, jnp.int32),
            pltpu.SMEM((n,), jnp.int32),
            pltpu.SMEM((n,), jnp.int32),
            pltpu.VMEM((layers, q_rows, width), sent),
            pltpu.VMEM((layers, k_rows, width), sent),
            pltpu.VMEM((n, layers, q_rows, LANES), sent),
            pltpu.VMEM((n, layers, k_rows, LANES), sent),
            pltpu.VMEM((half, 2, layers, q_rows, LANES), sent),
            pltpu.VMEM((half, 2, layers, k_rows, LANES), sent),
            pltpu.VMEM((n, 2, layers, q_rows, LANES), sent),
            pltpu.VMEM((n, 2, layers, k_rows, LANES), sent),
            pltpu.VMEM((2, layers, k_all, LANES), sent),
            pltpu.SemaphoreType.DMA((6,)),
            pltpu.SemaphoreType.DMA((n,)),
            pltpu.SemaphoreType.DMA((n,)),
            pltpu.SemaphoreType.DMA((n,)),
            pltpu.SemaphoreType.DMA((n,)),
        ],
        compiler_params=pltpu.CompilerParams(
            collective_id=0, has_side_effects=True, vmem_limit_bytes=64 * 2**20 - held - SPARE
        ),
    )(q_codes.transpose(1, 0, 2), k_codes.transpose(1, 0, 2), q_exps, k_exps, shard_of_host, head_owner)

    if q_rows % 16:
        order = jnp.arange(n, dtype=jnp.int32)
        holder = jnp.zeros((n,), jnp.int32).at[shard_of_host].set(order)
        filed = jnp.take(products, holder, axis=0)
        return filed.transpose(1, 2, 0, 3, 4).reshape(2, layers, q_all, k_all)
    return pl.pallas_call(
        functools.partial(place, n),
        out_shape=jax.ShapeDtypeStruct((2, layers, q_all, k_all), jnp.bfloat16),
        in_specs=[SMEM, VMEM],
        out_specs=HBM,
        scratch_shapes=[pltpu.SemaphoreType.DMA],
        compiler_params=pltpu.CompilerParams(vmem_limit_bytes=40 * 2**20),
    )(shard_of_host, products)


def solution(mesh):
    placed = (
        P("heads", "groups", None),
        P("heads", "groups", None),
        P("groups", None, None),
        P("groups", None, None),
        P(),
        P(),
    )
    return jax.shard_map(
        functools.partial(per_device, mesh.shape["heads"]),
        mesh=mesh,
        in_specs=placed,
        out_specs=P("heads", "groups", None, None),
        check_vma=False,
    )
```
